32 devices in a mesh: row: 4 (over z), col: 8 (over y, x, core).
Axes of the slice: x: 2, y: 2, z: 4, core: 2. Of those that a mesh axis runs over, the one named last changes fastest.
Arguments:
- points: bfloat16 [3, 12288], P(None, ('row', 'col')), as said below
- omega: bfloat16 [64, 12288], P(None, ('row', 'col')), may hold values from -6 to 6
- leaf_extra: int32 [32], replicated, may hold values from 1 to 769, 4128 in all
- owner_map: int32 [32], replicated, may hold values from 0 to 31, as said below
Outputs:
- samples: bfloat16 [64, 12288], P(None, ('row', 'col'))
- coupled: float32 [64, 4096], P(('row', 'col'))
The draws below stay inside these ranges and needn't reach their ends.
Inputs may be any that keep to these rules, and one draw needn't show every extreme that they name: `leaf_extra`: the values sum to 4128, and the largest is reached in every draw. `owner_map`: exactly 16 devices own 2 leaves each; the other devices own none. All coordinates lie in [0, 1]; the points fill the unit cube and are numbered in cluster tree order, so that points with near numbers lie near one another.
All inputs are finite; a program needn't handle non-finite values.
Results may differ from the reference program's by a relative error of at most 0.0037.
Values may be sent and summed in bfloat16 or wider, within the bound.
A program may use at most 128 MiB of HBM per device.

```python
import math
import jax
import jax.numpy as jnp
import numpy as np
from jax import lax

R = 64
LEAF_MIN = 256
LEAF_AVERAGE_SIZE = 384
LEAF_MAX = 1024
N = 12288
LEAVES = 32
SLOTS = 2
N_ROW = 4
N_COL = 8


def draw_points(key, part):
    jitter_key = jax.random.fold_in(key, 11)
    index = jnp.arange(N, dtype=jnp.int32)
    cell = index * 4096 // N
    coords = []
    for axis_id in range(3):
        level_sum = jnp.zeros((N,), jnp.int32)
        for level in range(4):
            level_sum = level_sum + (cell >> 3 * level + axis_id & 1) * (1 << level)
        coords.append(level_sum)
    cells = jnp.stack(coords, axis=0).astype(jnp.float32)
    jitter = jax.random.uniform(jitter_key, (3, N), jnp.float32)
    placed = (cells + jitter) / 16.0
    return placed.astype(jnp.bfloat16)


def draw_owner_map(key, part):
    owners = 2 * (LEAVES // SLOTS)
    devices = jax.random.permutation(jax.random.fold_in(key, 21), owners)
    order = jax.random.permutation(jax.random.fold_in(key, 22), LEAVES)
    return devices[order // SLOTS].astype(jnp.int32)


def levels(rng, shape, cuts, least, top_value):
    def one(dim, blocks):
        heights = jax.random.uniform(jax.random.fold_in(jax.random.fold_in(rng, 6), dim), (blocks,), jnp.float32, least / len(cuts), top_value / len(cuts))
        return jnp.repeat(jnp.exp(heights), shape[dim] // blocks).reshape((-1,) + (1,) * (len(shape) - dim - 1))

    level = one(*cuts[0])
    for cut in cuts[1:]:
        level = level * one(*cut)
    return level


def split_up(amount, total, bound, skew):
    portions = [(1 << 20) // math.isqrt(standing ** skew) + 1 for standing in range(2, amount + 1)]
    rest, given = total - bound - (amount - 1), [1] * (amount - 1)
    while rest > 0:
        candidates = [i for i in range(amount - 1) if given[i] < bound]
        mass, left = sum([portions[i] for i in candidates]), rest
        for i in candidates:
            addition = min(bound - given[i], max(1, left * portions[i] // mass), rest)
            given[i] = given[i] + addition
            rest = rest - addition
    return np.array([bound] + given)


def uneven_parts(stream_key, count, total, limit, lean):
    if count == 2:
        one = jax.random.randint(stream_key, (), max(1, total - limit), min(limit, total - 1) + 1)
        return jnp.stack([one, total - one])
    tallies = jnp.asarray(split_up(count, total, limit, lean), jnp.int32)
    twos = (count - 1) // 2
    source_of, sink = tallies[1:1 + 2 * twos:2], tallies[2:2 + 2 * twos:2]
    slack = jnp.minimum(source_of - 1, limit - sink)
    moved = jax.random.randint(jax.random.fold_in(stream_key, 1), (twos,), 0, 1 << 20) % (slack + 1)
    tallies = tallies.at[1:1 + 2 * twos:2].set(source_of - moved).at[2:2 + 2 * twos:2].set(sink + moved)
    return tallies[jax.random.permutation(jax.random.fold_in(stream_key, 2), count)]


def centred(own_key, dims, deviation, bound, cuts=(), kind=jnp.bfloat16):
    values = deviation * jax.random.normal(own_key, dims, jnp.float32)
    if cuts:
        values = values * levels(own_key, dims, cuts, -0.22, 0.18)
    return jnp.clip(values, -bound, bound).astype(kind)


def setup_inputs(seed: int = 0) -> dict:
    seeds = jax.random.split(jax.random.key(seed), 5)
    return {
        "points": draw_points(jax.random.fold_in(seeds[4], 71), 0),
        "omega": centred(seeds[1], (R, N), 1.0, 6.0, ((1, 32),)),
        "leaf_extra": uneven_parts(seeds[2], LEAVES, LEAVES * (LEAF_AVERAGE_SIZE - LEAF_MIN + 1), LEAF_MAX - LEAF_MIN + 1, 1).astype(jnp.int32),
        "owner_map": draw_owner_map(jax.random.fold_in(seeds[4], 71), 0),
    }


GAMMA = 8.0
SHIFT = 1.0
AMPC = 4.0

def kernel_tile(col_pts, row_pts, amp):
    first = col_pts[0][:, None] - row_pts[0][None, :]
    second = col_pts[1][:, None] - row_pts[1][None, :]
    third = col_pts[2][:, None] - row_pts[2][None, :]
    dist = first * first + second * second + third * third
    return amp * jnp.exp(-GAMMA * dist)

def lower_triangular_solver(factor, rhs, flip):
    return lax.linalg.triangular_solve(factor, rhs, left_side=True, lower=True, transpose_a=flip)

def leaf_coupling(ys, leaf_pts, valid, amp, ranks):
    gram = jnp.dot(ys, ys.T, precision=lax.Precision.HIGHEST)
    chol_g = jnp.linalg.cholesky(gram)
    basis_transposed = lower_triangular_solver(chol_g, ys, False)
    width = ys.shape[1]
    inner = jnp.where(valid[:, None] & valid[None, :], kernel_tile(leaf_pts, leaf_pts, amp), 0.0)
    dmat = inner + SHIFT * jnp.eye(width, dtype=jnp.float32)
    diagonal_cholesky_factor = jnp.linalg.cholesky(dmat)
    value_matrix = lower_triangular_solver(diagonal_cholesky_factor, basis_transposed.T, False)
    middle_matrix = jnp.dot(value_matrix.T, value_matrix, precision=lax.Precision.HIGHEST)
    chol_m = jnp.linalg.cholesky(middle_matrix)
    halfway = lower_triangular_solver(chol_m, jnp.eye(ranks, dtype=jnp.float32), False)
    inverse = lower_triangular_solver(chol_m, halfway, True)
    return inverse.reshape(ranks * ranks)

def reference(points, omega, leaf_extra, owner_map):
    n_all = points.shape[1]
    ranks = omega.shape[0]
    amp = AMPC / math.sqrt(n_all)
    pts = points.astype(jnp.float32)
    block = n_all if n_all <= 1024 else math.gcd(n_all, 1024)

    def one_block(begin):
        rows = lax.dynamic_slice_in_dim(pts, begin, block, 1)
        tile = kernel_tile(pts, rows, amp).astype(jnp.bfloat16)
        return jnp.dot(omega.astype(jnp.float32), tile.astype(jnp.float32), preferred_element_type=jnp.float32)
    begins = jnp.arange(n_all // block, dtype=jnp.int32) * block
    parts = lax.map(one_block, begins)
    total = jnp.transpose(parts, (1, 0, 2)).reshape(ranks, n_all)
    samples = (total + SHIFT * omega.astype(jnp.float32)).astype(jnp.bfloat16)
    sizes = leaf_extra + (LEAF_MIN - 1)
    starts = (jnp.cumsum(sizes) - sizes).astype(jnp.int32)
    samp_pad = jnp.concatenate([samples.astype(jnp.float32), jnp.zeros((ranks, LEAF_MAX), jnp.float32)], axis=1)
    pts_pad = jnp.concatenate([pts, jnp.zeros((3, LEAF_MAX), jnp.float32)], axis=1)
    offsets = jnp.arange(LEAF_MAX, dtype=jnp.int32)

    def per_leaf(args):
        begin, size = args
        valid = offsets < size
        ys = jnp.where(valid[None, :], lax.dynamic_slice_in_dim(samp_pad, begin, LEAF_MAX, 1), 0.0)
        leaf_pts = jnp.where(valid[None, :], lax.dynamic_slice_in_dim(pts_pad, begin, LEAF_MAX, 1), 0.0)
        return leaf_coupling(ys, leaf_pts, valid, amp, ranks)
    couplings = lax.map(per_leaf, (starts, sizes))
    leaf_ids = jnp.arange(LEAVES, dtype=jnp.int32)
    same = (owner_map[None, :] == owner_map[:, None]) & (leaf_ids[None, :] < leaf_ids[:, None])
    rank = lax.optimization_barrier(jnp.sum(same.astype(jnp.int32), axis=1))
    dest = (owner_map * SLOTS + rank).astype(jnp.int32)
    coupled = jnp.zeros((N_ROW * N_COL * SLOTS, ranks * ranks), jnp.float32).at[dest].set(couplings)
    return (samples, coupled)
```

```python
import functools
import math

import jax
import jax.numpy as jnp
from jax import lax
from jax.experimental import pallas as pl
from jax.experimental.pallas import tpu as pltpu
from jax.sharding import PartitionSpec as P

LEAF_MIN = 256
LEAF_MAX = 1024
SLOTS = 2
GAMMA = 8.0
SHIFT = 1.0
AMPC = 4.0

FEAT = 16
WINDOW = LEAF_MAX + 256
MAX_STEPS = 96
TOL = 1e-4
MESH = pl.DeviceIdType.MESH
VMEM = pltpu.MemorySpace.VMEM
SMEM = pltpu.MemorySpace.SMEM
F32 = jnp.float32
BF16 = jnp.bfloat16
SCALE = GAMMA * math.log2(math.e)


def three(value):
    high = value.astype(BF16).astype(F32)
    rest = value - high
    middle = rest.astype(BF16).astype(F32)
    low = (rest - middle).astype(BF16).astype(F32)
    return high, middle, low


def stack_rows(rows, width):
    ids = lax.broadcasted_iota(jnp.int32, (FEAT, width), 0)
    out = jnp.zeros((FEAT, width), F32)
    for spot, row in enumerate(rows):
        out = jnp.where(ids == spot, row, out)
    return out


def squares(p0, p1, p2):
    return p0 * p0 + p1 * p1 + p2 * p2


def left_features(p0, p1, p2):
    one = jnp.ones_like(p0)
    norms = three(-SCALE * squares(p0, p1, p2))
    return stack_rows([p0, p1, p2] * 3 + list(norms) + [one] * 3, p0.shape[1])


def right_features(p0, p1, p2, amp, valid):
    one = jnp.ones_like(p0)
    parts = [three(2.0 * SCALE * p) for p in (p0, p1, p2)]
    norm = math.log2(amp) - SCALE * squares(p0, p1, p2)
    if valid is not None:
        norm = jnp.where(valid, norm, -30000.0)
    rows = [parts[d][k] for k in range(3) for d in range(3)]
    return stack_rows(rows + [one] * 3 + list(three(norm)), p0.shape[1])


def fill_pack(omega_ref, pts_ref, dst):
    ranks = omega_ref.shape[0]
    pts = pts_ref[...].astype(F32)
    dst[0:ranks, :] = omega_ref[...]
    dst[ranks:ranks + FEAT, :] = left_features(pts[0:1], pts[1:2], pts[2:3]).astype(BF16)


def spread(block, send_sem, recv_sem):
    z, col = lax.axis_index("row"), lax.axis_index("col")
    y, x, core = col // 4, (col // 2) % 2, col % 2

    def at(zz, yy, xx, cc):
        return zz * 8 + yy * 4 + xx * 2 + cc

    zs = [lax.rem(z + d, 4) for d in range(4)]
    xn, yn, cn = (z, y * 4 + (1 - x) * 2 + core), (z, (1 - y) * 4 + x * 2 + core), (z, y * 4 + x * 2 + 1 - core)
    peers = [(zs[d], col) for d in (1, 3, 2)] + [xn, yn, cn]
    barrier = pltpu.get_barrier_semaphore()
    for peer in peers:
        pl.semaphore_signal(barrier, inc=1, device_id=peer, device_id_type=MESH)
    pl.semaphore_wait(barrier, len(peers))
    sent = []

    def send(index, to):
        copy = pltpu.make_async_remote_copy(
            src_ref=block(index), dst_ref=block(index),
            send_sem=send_sem.at[len(sent)], recv_sem=recv_sem.at[index],
            device_id=to, device_id_type=MESH,
        )
        copy.start()
        sent.append(copy)

    def receive(index):
        pltpu.make_async_remote_copy(
            src_ref=block(index), dst_ref=block(index),
            send_sem=send_sem.at[0], recv_sem=recv_sem.at[index],
            device_id=cn, device_id_type=MESH,
        ).wait_recv()

    mine = at(z, y, x, core)
    for peer in (xn, yn) + tuple(peers[:3]) + (cn,):
        send(mine, peer)
    for d in (1, 3, 2):
        got = at(zs[d], y, x, core)
        receive(got)
        for peer in (xn, yn, cn):
            send(got, peer)
    for d in (0, 1, 3, 2):
        via_x = at(zs[d], y, 1 - x, core)
        receive(via_x)
        if d < 2:
            send(via_x, yn)
        send(via_x, cn)
        via_y = at(zs[d], 1 - y, x, core)
        receive(via_y)
        if d >= 2:
            send(via_y, xn)
        send(via_y, cn)
    for d in (0, 1, 3, 2):
        far = at(zs[d], 1 - y, 1 - x, core)
        receive(far)
        send(far, cn)
    for d in (0, 1, 3, 2):
        receive(at(zs[d], y, x, 1 - core))
    for d in (0, 1, 3, 2):
        receive(at(zs[d], y, 1 - x, 1 - core))
        receive(at(zs[d], 1 - y, x, 1 - core))
    for d in (0, 1, 3, 2):
        receive(at(zs[d], 1 - y, 1 - x, 1 - core))
    for copy in sent:
        copy.wait_send()


def gather_pack_kernel(omega_ref, pts_ref, out_ref, send_sem, recv_sem):
    width = omega_ref.shape[1]

    def block(index):
        return out_ref.at[:, pl.ds(pl.multiple_of(index * width, 128), width)]

    device = lax.axis_index("row") * 8 + lax.axis_index("col")
    fill_pack(omega_ref, pts_ref, block(device))
    spread(block, send_sem, recv_sem)


def pack_kernel(omega_ref, pts_ref, out_ref):
    fill_pack(omega_ref, pts_ref, out_ref)


def owned(owner_ref, device, slot):
    seen, leaf = jnp.int32(0), jnp.int32(-1)
    for index in range(owner_ref.shape[0]):
        hit = (owner_ref[index] == device).astype(jnp.int32)
        take = hit * (seen == slot).astype(jnp.int32)
        leaf = leaf + take * (index - leaf)
        seen = seen + hit
    return leaf


def gather_coupling_kernel(owner_ref, block_ref, out_ref, buf, send_sem, recv_sem):
    device = lax.axis_index("row") * 8 + lax.axis_index("col")
    buf[device] = block_ref[...]
    spread(lambda index: buf.at[index], send_sem, recv_sem)
    for slot in range(SLOTS):
        leaf = owned(owner_ref, device, slot)
        found = buf[jnp.maximum(leaf, 0)]
        out_ref[slot] = jnp.where(leaf >= 0, found, 0.0)


def pick_kernel(where_ref, owner_ref, every_ref, out_ref):
    for slot in range(SLOTS):
        leaf = owned(owner_ref, where_ref[0], slot)
        found = every_ref[jnp.maximum(leaf, 0)]
        out_ref[slot] = jnp.where(leaf >= 0, found, 0.0)


def rolled(window, shift):
    return pltpu.roll(window, WINDOW - shift, 1)


def leaf_kernel(where_ref, extra_ref, g_ref, samp_ref, coup_ref, q_ref, acc_ref, k_ref, x_ref, r_ref, p_ref, *, amp, per_dev):
    ranks, total = samp_ref.shape[0], g_ref.shape[1]
    device = where_ref[0]

    def scan(index, carry):
        begin, size = carry
        now = extra_ref[index] + (LEAF_MIN - 1)
        begin = begin + jnp.where(index < device, now, 0)
        return begin, jnp.where(index == device, now, size)

    start, size = lax.fori_loop(0, extra_ref.shape[0], scan, (jnp.int32(0), jnp.int32(0)))
    base = pl.multiple_of(jnp.minimum((start // 128) * 128, total - WINDOW), 128)
    shift = start - base
    own = pl.multiple_of(device * per_dev, 128)

    valid = lax.broadcasted_iota(jnp.int32, (1, LEAF_MAX), 1) < size
    pts = rolled(g_ref[ranks:ranks + FEAT, pl.ds(base, WINDOW)].astype(F32), shift)[:, :LEAF_MAX]
    feats = right_features(pts[0:1], pts[1:2], pts[2:3], amp, valid)
    q_ref[0:LEAF_MAX, :] = feats.T.astype(BF16)
    leaf_left = left_features(pts[0:1], pts[1:2], pts[2:3])
    leaf_left = jnp.where(valid, leaf_left, 0.0)
    ids = lax.broadcasted_iota(jnp.int32, (FEAT, LEAF_MAX), 0)
    leaf_left = jnp.where(valid | (ids != 9), leaf_left, -30000.0).astype(BF16)
    mine = g_ref[ranks:ranks + FEAT, pl.ds(own, per_dev)].astype(F32)
    feats = right_features(mine[0:1], mine[1:2], mine[2:3], amp, None)
    q_ref[LEAF_MAX:LEAF_MAX + per_dev, :] = feats.T.astype(BF16)

    acc_ref[...] = jnp.zeros_like(acc_ref)
    count = LEAF_MAX + per_dev
    chunk = 512

    def step(outer, carry):
        at = pl.multiple_of(outer * chunk, 128)
        left = g_ref[ranks:ranks + FEAT, pl.ds(at, chunk)]
        omega = g_ref[0:ranks, pl.ds(at, chunk)]
        for low in range(0, count, 256):
            high = min(low + 256, count)
            power = jnp.dot(q_ref[low:high, :], left, preferred_element_type=F32)
            tile = jnp.exp2(power).astype(BF16)
            acc_ref[:, low:high] += lax.dot_general(
                omega, tile, (((1,), (1,)), ((), ())), preferred_element_type=F32)
        return carry

    lax.fori_loop(0, total // chunk, step, 0)

    mine = g_ref[0:ranks, pl.ds(own, per_dev)].astype(F32)
    samp_ref[...] = (acc_ref[:, LEAF_MAX:] + SHIFT * mine).astype(BF16)
    mine = rolled(g_ref[0:ranks, pl.ds(base, WINDOW)].astype(F32), shift)[:, :LEAF_MAX]
    y16 = jnp.where(valid, acc_ref[:, :LEAF_MAX] + SHIFT * mine, 0.0).astype(BF16)
    ys = y16.astype(F32)

    for low in range(0, LEAF_MAX, 256):
        power = jnp.dot(q_ref[low:low + 256, :], leaf_left, preferred_element_type=F32)
        k_ref[low:low + 256, :] = jnp.exp2(power).astype(BF16)

    x_ref[...] = jnp.zeros_like(x_ref)
    r_ref[...] = ys
    p_ref[...] = ys
    norm0 = jnp.sum(ys * ys, axis=1, keepdims=True)

    def going(carry):
        index, worst, _ = carry
        return (index < MAX_STEPS) & (worst > TOL * TOL)

    def iterate(carry):
        index, _, norm = carry
        p = p_ref[...]
        high = p.astype(BF16)
        low = (p - high.astype(F32)).astype(BF16)
        both = jnp.dot(jnp.concatenate([high, low], axis=0), k_ref[...], preferred_element_type=F32)
        dp = SHIFT * p + both[:ranks] + both[ranks:]
        energy = jnp.sum(p * dp, axis=1, keepdims=True)
        alpha = jnp.where(energy > 0.0, norm / energy, 0.0)
        x_ref[...] += alpha * p
        r = r_ref[...] - alpha * dp
        r_ref[...] = r
        fresh = jnp.sum(r * r, axis=1, keepdims=True)
        p_ref[...] = r + jnp.where(norm > 0.0, fresh / norm, 0.0) * p
        worst = jnp.max(jnp.where(norm0 > 0.0, fresh / norm0, 0.0))
        return index + 1, worst, fresh

    lax.while_loop(going, iterate, (jnp.int32(0), F32(1.0), norm0))

    nt = (((1,), (1,)), ((), ()))
    exact = dict(precision=lax.Precision.HIGHEST, preferred_element_type=F32)
    x = x_ref[...]
    inner = lax.dot_general(ys, x, nt, **exact) + lax.dot_general(x, r_ref[...], nt, **exact)
    gram = lax.dot_general(y16, y16, nt, preferred_element_type=F32)
    rows = lax.broadcasted_iota(jnp.int32, (ranks, 1), 0)
    cols = lax.broadcasted_iota(jnp.int32, (1, ranks), 1)
    eye = jnp.where(rows == cols, 1.0, 0.0).astype(F32)

    left = jnp.concatenate([inner, eye], axis=1)
    right = gram
    dinv = jnp.ones((ranks, 1), F32)
    root = jnp.ones((ranks, 1), F32)
    for k in range(ranks):
        a, b = left[k:k + 1, :], right[k:k + 1, :]
        ainv, binv = 1.0 / a[:, k:k + 1], 1.0 / b[:, k:k + 1]
        below = rows > k
        left = left - jnp.where(below, left[:, k:k + 1] * ainv, 0.0) * a
        right = right - jnp.where(below, right[:, k:k + 1] * binv, 0.0) * b
        dinv = jnp.where(rows == k, ainv, dinv)
        root = jnp.where(rows == k, jnp.sqrt(binv), root)
    upper = jnp.where(cols >= rows, right * root, 0.0)
    mid = lax.dot_general(left[:, ranks:], upper, nt, **exact)
    coup = lax.dot_general(mid, mid * dinv, (((0,), (0,)), ((), ())), **exact)
    half = ranks // 2
    coup_ref[:, :ranks] = coup[:half]
    coup_ref[:, ranks:] = coup[half:]


def shards(points, omega, leaf_extra, owner_map):
    ranks, per_dev = omega.shape
    n_row, n_col = lax.axis_size("row"), lax.axis_size("col")
    n_dev = n_row * n_col
    n_all = per_dev * n_dev
    amp = AMPC / math.sqrt(n_all)
    device = lax.axis_index(("row", "col"))
    block = (ranks // 2, 2 * ranks)
    small = (n_row, n_col) == (4, 8)
    vm = pl.BlockSpec(memory_space=VMEM)
    sm = pl.BlockSpec(memory_space=SMEM)
    sems = [pltpu.SemaphoreType.DMA((31,)), pltpu.SemaphoreType.DMA((32,))]
    if small:
        pack = pl.pallas_call(
            gather_pack_kernel,
            out_shape=jax.ShapeDtypeStruct((ranks + FEAT, n_all), BF16),
            in_specs=[vm, vm], out_specs=vm, scratch_shapes=sems,
            compiler_params=pltpu.CompilerParams(collective_id=0, has_side_effects=True, vmem_limit_bytes=24 << 20),
        )(omega, points)
    else:
        pack = pl.pallas_call(
            pack_kernel,
            out_shape=jax.ShapeDtypeStruct((ranks + FEAT, per_dev), BF16),
            in_specs=[vm, vm], out_specs=vm,
        )(omega, points)
        pack = lax.all_gather(pack, ("row", "col"), axis=1, tiled=True)
    samples, coup = pl.pallas_call(
        functools.partial(leaf_kernel, amp=amp, per_dev=per_dev),
        out_shape=(jax.ShapeDtypeStruct((ranks, per_dev), BF16), jax.ShapeDtypeStruct(block, F32)),
        in_specs=[sm, sm, vm], out_specs=(vm, vm),
        scratch_shapes=[
            pltpu.VMEM((LEAF_MAX + per_dev, FEAT), BF16),
            pltpu.VMEM((ranks, LEAF_MAX + per_dev), F32),
            pltpu.VMEM((LEAF_MAX, LEAF_MAX), BF16),
            pltpu.VMEM((ranks, LEAF_MAX), F32),
            pltpu.VMEM((ranks, LEAF_MAX), F32),
            pltpu.VMEM((ranks, LEAF_MAX), F32),
        ],
        compiler_params=pltpu.CompilerParams(vmem_limit_bytes=48 << 20),
    )(device.astype(jnp.int32).reshape(1), leaf_extra, pack)
    if small:
        mine = pl.pallas_call(
            gather_coupling_kernel,
            out_shape=jax.ShapeDtypeStruct((SLOTS,) + block, F32),
            in_specs=[sm, vm], out_specs=vm,
            scratch_shapes=[pltpu.VMEM((n_dev,) + block, F32)] + sems,
            compiler_params=pltpu.CompilerParams(collective_id=1, has_side_effects=True),
        )(owner_map, coup)
    else:
        every = lax.all_gather(coup, ("row", "col"), axis=0)
        mine = pl.pallas_call(
            pick_kernel,
            out_shape=jax.ShapeDtypeStruct((SLOTS,) + block, F32),
            in_specs=[sm, sm, vm], out_specs=vm,
        )(device.astype(jnp.int32).reshape(1), owner_map, every)
    coupled = mine.reshape(SLOTS, ranks // 2, 2, ranks).transpose(0, 2, 1, 3).reshape(SLOTS, ranks * ranks)
    return samples, coupled


def solution(mesh):
    return jax.shard_map(
        shards,
        mesh=mesh,
        in_specs=(P(None, ("row", "col")), P(None, ("row", "col")), P(), P()),
        out_specs=(P(None, ("row", "col")), P(("row", "col"), None)),
        check_vma=False,
    )
```

```python
import functools
import math

import jax
import jax.numpy as jnp
from jax import lax
from jax.experimental import pallas as pl
from jax.experimental.pallas import tpu as pltpu
from jax.sharding import PartitionSpec as P

LEAF_MIN = 256
LEAF_MAX = 1024
SLOTS = 2
GAMMA = 8.0
SHIFT = 1.0
AMPC = 4.0

FEAT = 16
WINDOW = LEAF_MAX + 256
MAX_STEPS = 96
PART = 256
JCHUNK = 4096
TOL = 1e-4
MESH = pl.DeviceIdType.MESH
VMEM = pltpu.MemorySpace.VMEM
SMEM = pltpu.MemorySpace.SMEM
F32 = jnp.float32
BF16 = jnp.bfloat16
SCALE = GAMMA * math.log2(math.e)


def three(value):
    high = value.astype(BF16).astype(F32)
    rest = value - high
    middle = rest.astype(BF16).astype(F32)
    low = (rest - middle).astype(BF16).astype(F32)
    return high, middle, low


def stack_rows(rows, width):
    ids = lax.broadcasted_iota(jnp.int32, (FEAT, width), 0)
    out = jnp.zeros((FEAT, width), F32)
    for spot, row in enumerate(rows):
        out = jnp.where(ids == spot, row, out)
    return out


def squares(p0, p1, p2):
    return p0 * p0 + p1 * p1 + p2 * p2


def left_features(p0, p1, p2):
    one = jnp.ones_like(p0)
    norms = three(-SCALE * squares(p0, p1, p2))
    return stack_rows([p0, p1, p2] * 3 + list(norms) + [one] * 3, p0.shape[1])


def right_features(p0, p1, p2, amp, valid):
    one = jnp.ones_like(p0)
    parts = [three(2.0 * SCALE * p) for p in (p0, p1, p2)]
    norm = math.log2(amp) - SCALE * squares(p0, p1, p2)
    if valid is not None:
        norm = jnp.where(valid, norm, -30000.0)
    rows = [parts[d][k] for k in range(3) for d in range(3)]
    return stack_rows(rows + [one] * 3 + list(three(norm)), p0.shape[1])


def fill_pack(omega_ref, pts_ref, dst):
    ranks = omega_ref.shape[0]
    pts = pts_ref[...].astype(F32)
    dst[0:ranks, :] = omega_ref[...]
    dst[ranks:ranks + FEAT, :] = left_features(pts[0:1], pts[1:2], pts[2:3]).astype(BF16)


def spread(block, send_sem, recv_sem):
    z, col = lax.axis_index("row"), lax.axis_index("col")
    y, x, core = col // 4, (col // 2) % 2, col % 2

    def at(zz, yy, xx, cc):
        return zz * 8 + yy * 4 + xx * 2 + cc

    zs = [lax.rem(z + d, 4) for d in range(4)]
    xn, yn, cn = (z, y * 4 + (1 - x) * 2 + core), (z, (1 - y) * 4 + x * 2 + core), (z, y * 4 + x * 2 + 1 - core)
    peers = [(zs[d], col) for d in (1, 3, 2)] + [xn, yn, cn]
    barrier = pltpu.get_barrier_semaphore()
    for peer in peers:
        pl.semaphore_signal(barrier, inc=1, device_id=peer, device_id_type=MESH)
    pl.semaphore_wait(barrier, len(peers))
    sent = []

    def send(index, to):
        copy = pltpu.make_async_remote_copy(
            src_ref=block(index), dst_ref=block(index),
            send_sem=send_sem.at[len(sent)], recv_sem=recv_sem.at[index],
            device_id=to, device_id_type=MESH,
        )
        copy.start()
        sent.append(copy)

    def receive(index):
        pltpu.make_async_remote_copy(
            src_ref=block(index), dst_ref=block(index),
            send_sem=send_sem.at[0], recv_sem=recv_sem.at[index],
            device_id=cn, device_id_type=MESH,
        ).wait_recv()

    mine = at(z, y, x, core)
    for peer in (xn, yn) + tuple(peers[:3]) + (cn,):
        send(mine, peer)
    for d in (1, 3, 2):
        got = at(zs[d], y, x, core)
        receive(got)
        for peer in (xn, yn, cn):
            send(got, peer)
    for d in (0, 1, 3, 2):
        via_x = at(zs[d], y, 1 - x, core)
        receive(via_x)
        if d < 2:
            send(via_x, yn)
        send(via_x, cn)
        via_y = at(zs[d], 1 - y, x, core)
        receive(via_y)
        if d >= 2:
            send(via_y, xn)
        send(via_y, cn)
    for d in (0, 1, 3, 2):
        far = at(zs[d], 1 - y, 1 - x, core)
        receive(far)
        send(far, cn)
    for d in (0, 1, 3, 2):
        receive(at(zs[d], y, x, 1 - core))
    for d in (0, 1, 3, 2):
        receive(at(zs[d], y, 1 - x, 1 - core))
        receive(at(zs[d], 1 - y, x, 1 - core))
    for d in (0, 1, 3, 2):
        receive(at(zs[d], 1 - y, 1 - x, 1 - core))
    for copy in sent:
        copy.wait_send()


def gather_pack_kernel(omega_ref, pts_ref, out_ref, send_sem, recv_sem):
    width = omega_ref.shape[1]

    def block(index):
        return out_ref.at[:, pl.ds(pl.multiple_of(index * width, 128), width)]

    device = lax.axis_index("row") * 8 + lax.axis_index("col")
    fill_pack(omega_ref, pts_ref, block(device))
    spread(block, send_sem, recv_sem)


def pack_kernel(omega_ref, pts_ref, out_ref):
    fill_pack(omega_ref, pts_ref, out_ref)


def rolled(window, shift):
    return pltpu.roll(window, WINDOW - shift, 1)


def slots_of(owner_ref, extra_ref, device):
    def scan(index, carry):
        begin, seen, found = carry
        size = extra_ref[index] + (LEAF_MIN - 1)
        hit = owner_ref[index] == device
        found = tuple(
            (jnp.where(hit & (seen == slot), begin, old[0]), jnp.where(hit & (seen == slot), size, old[1]))
            for slot, old in enumerate(found)
        )
        return begin + size, seen + hit.astype(jnp.int32), found

    zero = jnp.int32(0)
    return lax.fori_loop(0, owner_ref.shape[0], scan, (zero, zero, ((zero, zero),) * SLOTS))[2]


def leaf_kernel(where_ref, owner_ref, extra_ref, g_ref, samp_ref, coup_ref, q_ref, left_ref, turned_ref, acc_ref, k_ref,
                x_ref, r_ref, p_ref, inner_ref, gram_ref, out_ref, *, amp, per_dev):
    ranks, total = samp_ref.shape[0], g_ref.shape[1]
    device = where_ref[0]
    leaves = slots_of(owner_ref, extra_ref, device)
    own = pl.multiple_of(device * per_dev, 128)
    own_at = SLOTS * LEAF_MAX
    nt = (((1,), (1,)), ((), ()))
    exact = dict(precision=lax.Precision.HIGHEST, preferred_element_type=F32)

    def window(slot):
        start, size = leaves[slot]
        base = pl.multiple_of(jnp.minimum((start // 128) * 128, total - WINDOW), 128)
        return base, start - base, lax.broadcasted_iota(jnp.int32, (1, LEAF_MAX), 1) < size

    for slot in range(SLOTS):
        @pl.when(leaves[slot][1] > 0)
        def _():
            base, shift, valid = window(slot)
            pts = rolled(g_ref[ranks:ranks + FEAT, pl.ds(base, WINDOW)].astype(F32), shift)[:, :LEAF_MAX]
            feats = right_features(pts[0:1], pts[1:2], pts[2:3], amp, valid)
            q_ref[:, slot * LEAF_MAX:(slot + 1) * LEAF_MAX] = feats.astype(BF16)
            mirror = jnp.where(valid, left_features(pts[0:1], pts[1:2], pts[2:3]), 0.0)
            ids = lax.broadcasted_iota(jnp.int32, (FEAT, LEAF_MAX), 0)
            left_ref[slot] = jnp.where(valid | (ids != 9), mirror, -30000.0).T.astype(BF16)

    mine = g_ref[ranks:ranks + FEAT, pl.ds(own, per_dev)].astype(F32)
    feats = right_features(mine[0:1], mine[1:2], mine[2:3], amp, None)
    q_ref[:, own_at:own_at + per_dev] = feats.astype(BF16)

    chunk = math.gcd(total, JCHUNK)

    def sample(points):
        def step(outer, acc):
            at = pl.multiple_of(outer * chunk, 128)
            power = jnp.dot(turned_ref[pl.ds(at, chunk), :], points, preferred_element_type=F32)
            tile = jnp.exp2(power).astype(BF16)
            return acc + jnp.dot(g_ref[0:ranks, pl.ds(at, chunk)], tile, preferred_element_type=F32)

        return lax.fori_loop(0, total // chunk, step, jnp.zeros((ranks, points.shape[1]), F32))

    turn = math.gcd(total, 1024)

    def transpose(index, carry):
        at = pl.multiple_of(index * turn, 128)
        turned_ref[pl.ds(at, turn), :] = g_ref[ranks:ranks + FEAT, pl.ds(at, turn)].astype(F32).T.astype(BF16)
        return carry

    lax.fori_loop(0, total // turn, transpose, 0)

    mine = g_ref[0:ranks, pl.ds(own, per_dev)].astype(F32)
    samp_ref[...] = (sample(q_ref[:, own_at:own_at + per_dev]) + SHIFT * mine).astype(BF16)

    counts = [(leaves[slot][1] + PART - 1) // PART for slot in range(SLOTS)]

    def part(index, carry):
        at = jnp.where(index < counts[0], index * PART, LEAF_MAX + (index - counts[0]) * PART)
        at = pl.multiple_of(at, PART)
        acc_ref[:, pl.ds(at, PART)] = sample(q_ref[:, pl.ds(at, PART)])
        return carry

    lax.fori_loop(0, counts[0] + counts[1], part, 0)

    def solve(slot, n):
        base, shift, valid = window(slot)
        mine = rolled(g_ref[0:ranks, pl.ds(base, WINDOW)].astype(F32), shift)[:, :n]
        total_y = acc_ref[:, slot * LEAF_MAX:slot * LEAF_MAX + n] + SHIFT * mine
        y16 = jnp.where(valid[:, :n], total_y, 0.0).astype(BF16)
        ys = y16.astype(F32)

        for low in range(0, n, 256):
            q = q_ref[:, slot * LEAF_MAX:slot * LEAF_MAX + n]
            power = jnp.dot(left_ref[slot, low:low + 256, :], q, preferred_element_type=F32)
            k_ref[low:low + 256, :n] = jnp.exp2(power).astype(BF16)

        x_ref[:, :n] = jnp.zeros((ranks, n), F32)
        r_ref[:, :n] = ys
        p_ref[:, :n] = ys
        norm0 = jnp.sum(ys * ys, axis=1, keepdims=True)

        def going(carry):
            index, worst, _ = carry
            return (index < MAX_STEPS) & (worst > TOL * TOL)

        def iterate(carry):
            index, _, norm = carry
            p = p_ref[:, :n]
            high = p.astype(BF16)
            low = (p - high.astype(F32)).astype(BF16)
            both = jnp.dot(jnp.concatenate([high, low], axis=0), k_ref[:n, :n], preferred_element_type=F32)
            dp = SHIFT * p + both[:ranks] + both[ranks:]
            energy = jnp.sum(p * dp, axis=1, keepdims=True)
            alpha = jnp.where(energy > 0.0, norm / energy, 0.0)
            x_ref[:, :n] += alpha * p
            r = r_ref[:, :n] - alpha * dp
            r_ref[:, :n] = r
            fresh = jnp.sum(r * r, axis=1, keepdims=True)
            p_ref[:, :n] = r + jnp.where(norm > 0.0, fresh / norm, 0.0) * p
            worst = jnp.max(jnp.where(norm0 > 0.0, fresh / norm0, 0.0))
            return index + 1, worst, fresh

        lax.while_loop(going, iterate, (jnp.int32(0), F32(1.0), norm0))
        x = x_ref[:, :n]
        inner_ref[slot] = lax.dot_general(ys, x, nt, **exact) + lax.dot_general(x, r_ref[:, :n], nt, **exact)
        gram_ref[slot] = lax.dot_general(y16, y16, nt, preferred_element_type=F32)

    for slot in range(SLOTS):
        size = leaves[slot][1]
        for under, n in ((0, LEAF_MAX // 2), (LEAF_MAX // 2, LEAF_MAX)):
            @pl.when((size > under) & (size <= n))
            def _():
                solve(slot, n)

    coup_ref[...] = jnp.zeros_like(coup_ref)

    @pl.when(leaves[0][1] > 0)
    def _():
        rows = lax.broadcasted_iota(jnp.int32, (ranks, 1), 0)
        cols = lax.broadcasted_iota(jnp.int32, (1, ranks), 1)
        eye = jnp.where(rows == cols, 1.0, 0.0).astype(F32)
        state = [
            [jnp.concatenate([inner_ref[slot], eye], axis=1), gram_ref[slot], jnp.ones((ranks, 1), F32), jnp.ones((ranks, 1), F32)]
            for slot in range(SLOTS)
        ]
        for k in range(ranks):
            below = rows > k
            for item in state:
                left, right, dinv, root = item
                a, b = left[k:k + 1, :], right[k:k + 1, :]
                ainv, binv = 1.0 / a[:, k:k + 1], 1.0 / b[:, k:k + 1]
                item[0] = left - jnp.where(below, left[:, k:k + 1] * ainv, 0.0) * a
                item[1] = right - jnp.where(below, right[:, k:k + 1] * binv, 0.0) * b
                item[2] = jnp.where(rows == k, ainv, dinv)
                item[3] = jnp.where(rows == k, jnp.sqrt(binv), root)
        for slot, (left, right, dinv, root) in enumerate(state):
            @pl.when(leaves[slot][1] > 0)
            def _():
                upper = jnp.where(cols >= rows, right * root, 0.0)
                mid = lax.dot_general(left[:, ranks:], upper, nt, **exact)
                out_ref[...] = lax.dot_general(mid, mid * dinv, (((0,), (0,)), ((), ())), **exact)
                half = ranks // 2
                pairs = jnp.concatenate(
                    [out_ref[pl.ds(0, half, stride=2), :], out_ref[pl.ds(1, half, stride=2), :]], axis=1)
                for row in range(half):
                    at = row * 2 * ranks
                    coup_ref[slot:slot + 1, at:at + 2 * ranks] = pairs[row:row + 1, :]


def shards(points, omega, leaf_extra, owner_map):
    ranks, per_dev = omega.shape
    n_row, n_col = lax.axis_size("row"), lax.axis_size("col")
    n_dev = n_row * n_col
    n_all = per_dev * n_dev
    amp = AMPC / math.sqrt(n_all)
    device = lax.axis_index(("row", "col"))
    small = (n_row, n_col) == (4, 8)
    vm = pl.BlockSpec(memory_space=VMEM)
    sm = pl.BlockSpec(memory_space=SMEM)
    sems = [pltpu.SemaphoreType.DMA((31,)), pltpu.SemaphoreType.DMA((32,))]
    if small:
        pack = pl.pallas_call(
            gather_pack_kernel,
            out_shape=jax.ShapeDtypeStruct((ranks + FEAT, n_all), BF16),
            in_specs=[vm, vm], out_specs=vm, scratch_shapes=sems,
            compiler_params=pltpu.CompilerParams(collective_id=0, has_side_effects=True, vmem_limit_bytes=24 << 20),
        )(omega, points)
    else:
        pack = pl.pallas_call(
            pack_kernel,
            out_shape=jax.ShapeDtypeStruct((ranks + FEAT, per_dev), BF16),
            in_specs=[vm, vm], out_specs=vm,
        )(omega, points)
        pack = lax.all_gather(pack, ("row", "col"), axis=1, tiled=True)
    return pl.pallas_call(
        functools.partial(leaf_kernel, amp=amp, per_dev=per_dev),
        out_shape=(
            jax.ShapeDtypeStruct((ranks, per_dev), BF16),
            jax.ShapeDtypeStruct((SLOTS, ranks * ranks), F32),
        ),
        in_specs=[sm, sm, sm, vm], out_specs=(vm, vm),
        scratch_shapes=[
            pltpu.VMEM((FEAT, SLOTS * LEAF_MAX + per_dev), BF16),
            pltpu.VMEM((SLOTS, LEAF_MAX, FEAT), BF16),
            pltpu.VMEM((n_all, FEAT), BF16),
            pltpu.VMEM((ranks, SLOTS * LEAF_MAX), F32),
            pltpu.VMEM((LEAF_MAX, LEAF_MAX), BF16),
            pltpu.VMEM((ranks, LEAF_MAX), F32),
            pltpu.VMEM((ranks, LEAF_MAX), F32),
            pltpu.VMEM((ranks, LEAF_MAX), F32),
            pltpu.VMEM((SLOTS, ranks, ranks), F32),
            pltpu.VMEM((SLOTS, ranks, ranks), F32),
            pltpu.VMEM((ranks, ranks), F32),
        ],
        compiler_params=pltpu.CompilerParams(vmem_limit_bytes=48 << 20),
    )(device.astype(jnp.int32).reshape(1), owner_map, leaf_extra, pack)


def solution(mesh):
    return jax.shard_map(
        shards,
        mesh=mesh,
        in_specs=(P(None, ("row", "col")), P(None, ("row", "col")), P(), P()),
        out_specs=(P(None, ("row", "col")), P(("row", "col"), None)),
        check_vma=False,
    )
```
